1024 devices in a mesh: dp: 16 (over y, core), expert: 16 (over z), head: 4 (over x).
Axes of the slice: x: 4, y: 8, z: 16, core: 2. Of those that a mesh axis runs over, the one named last changes fastest.
Arguments:
- tokens: bfloat16 [32768, 4096], P(('dp', 'expert')), may hold values from -6 to 6
- routes: int32 [32768, 8], P(('dp', 'expert')), may hold values from 0 to 127, all different within a row; in each aligned block of 128 rows (0 to 127, 128 to 255, ...) at most 16 rows name the same one
- route_weights: float32 [32768, 8], P(('dp', 'expert')), may hold values from 0.05 to 1
- gate_weight: bfloat16 [16, 4096, 1024], P('expert', None, 'head'), may hold values from -0.09375 to 0.09375
- up_weight: bfloat16 [16, 4096, 1024], P('expert', None, 'head'), may hold values from -0.09375 to 0.09375
- down_weight: bfloat16 [16, 1024, 4096], P('expert', 'head', 'dp'), may hold values from -0.1875 to 0.1875
Outputs:
- combined: bfloat16 [32768, 4096], P(('dp', 'expert'), 'head')
The draws below stay inside these ranges and needn't reach their ends.
Inputs may be any that keep to these rules, and one draw needn't show every extreme that they name: `routes`: each row names 8 different experts; among the 128 rows of one device, no expert is named by more than 16 rows, a bound that some block reaches.
All inputs are finite; a program needn't handle non-finite values.
Results may differ from the reference program's by a relative error of at most 0.017.
Values may be sent and summed in bfloat16 or wider, within the bound.
A program may use at most 64 MiB of HBM per device.

```python
import math
import jax
import jax.numpy as jnp
import numpy as np
from jax import lax

D = 4096
FF = 1024
EXPERTS = 128
TOP = 8
TOK_DEV = 128
CAP = 16
EXP_LOCAL = 8
FLIGHT = 16
TOKENS = 32768
N_HEAD = 4


def shard_levels(stream_key, extent, cuts, least, high):
    gain = 1.0
    for dim, blocks in cuts:
        draws = jax.random.uniform(jax.random.fold_in(jax.random.fold_in(stream_key, 6), dim), (blocks,), jnp.float32, least / len(cuts), high / len(cuts))
        gain = gain * jnp.repeat(jnp.exp(draws), extent[dim] // blocks).reshape((-1,) + (1,) * (len(extent) - 1 - dim))
    return gain


def assign_block(stream_key, own, number, rows, number_of, top, most, skew):
    ranking = jax.random.permutation(stream_key, number_of)
    crowded, usual = portions_of(number_of, rows * top, most, skew, True), portions_of(number_of, rows * top, most, skew, False)
    places = jnp.arange(number_of)

    def named(tallies, turn):
        used = int((tallies > 0).sum())
        fixed = max(1, used // 4)
        moved = fixed + (places - fixed + turn * (used - fixed)) % max(1, number_of - fixed)
        return jnp.zeros((number_of,), jnp.int32).at[ranking[jnp.where(places < fixed, places, moved)]].set(jnp.asarray(tallies, jnp.int32))

    tallies = jnp.where(number % 4 == 0, named(crowded, number // 4), named(usual, number - number // 4 - 1))
    mixed = jax.random.permutation(jax.random.fold_in(own, 3), number_of)
    source_of, sink = mixed[0:number_of // 2 * 2:2], mixed[1:number_of // 2 * 2:2]
    room = jnp.minimum(tallies[source_of] - 1, most - tallies[sink]) // 2
    room = jnp.where((source_of == ranking[0]) | (sink == ranking[0]) | (tallies[sink] == 0), 0, jnp.maximum(room, 0))
    moved = jax.random.randint(jax.random.fold_in(own, 4), (number_of // 2,), 0, 1 << 20) % (room + 1)
    tallies = tallies.at[source_of].add(-moved).at[sink].add(moved)
    labels = jnp.searchsorted(jnp.cumsum(tallies), jnp.arange(rows * top), side="right").astype(jnp.int32)
    grid = labels.reshape(top, rows).T
    grid = grid[jax.random.permutation(jax.random.fold_in(own, 1), rows)]
    turn = jax.random.randint(jax.random.fold_in(own, 2), (rows, 1), 0, top)
    return jnp.take_along_axis(grid, (jnp.arange(top)[None, :] + turn) % top, axis=1)


def portions_of(count, total, bound, skew, full):
    portions = [(1 << 20) // math.isqrt(grade ** skew) + 1 for grade in range(1, count + 1)]
    largest = bound if full else min(bound, max(-(-total // count), total * portions[0] // sum(portions)))
    least = 1 if total - largest >= count - 1 else 0
    holding, spare = [largest] + [least] * (count - 1), total - largest - least * (count - 1)
    while spare > 0:
        free = [i for i in range(1, count) if holding[i] < largest] or [i for i in range(1, count) if holding[i] < bound]
        whole, left = sum([portions[i] for i in free]), spare
        for i in free:
            extra = min(bound - holding[i], max(1, left * portions[i] // whole), spare)
            holding[i] = holding[i] + extra
            spare = spare - extra
    return np.array(holding)


def centred(key, dims, width, reach, split=(), kind=jnp.bfloat16):
    gain = shard_levels(key, dims, split, -0.22, 0.18) if split else 1.0
    result = jax.random.normal(key, dims, jnp.float32) * width * gain
    return jnp.minimum(jnp.maximum(result, -reach), reach).astype(kind)


def setup_inputs(seed: int = 0) -> dict:
    seeds = jax.random.split(jax.random.key(seed), 7)
    tokens = centred(seeds[0], (TOKENS, D), 1.0, 6.0, ((0, 256),))
    routes_keys = jax.random.split(jax.random.fold_in(seeds[1], 1), TOKENS // TOK_DEV)
    routes_turns = jax.random.permutation(jax.random.fold_in(seeds[1], 3), TOKENS // TOK_DEV)
    routes = jax.vmap(lambda own, number: assign_block(jax.random.fold_in(seeds[1], 2), own, number, TOK_DEV, EXPERTS, TOP, CAP, 2))(routes_keys, routes_turns).reshape((TOKENS, TOP))
    route_weights = jnp.clip(jnp.exp(math.log(1.0) - 2.9957323 * jax.random.uniform(seeds[2], (TOKENS, TOP), jnp.float32) ** shard_levels(seeds[2], (TOKENS, TOP), ((0, 256),), -0.2, 0.2)), 0.05, 1.0)
    gate_weight = centred(seeds[3], (FLIGHT, D, FF), D ** -0.5, 0.09375, ((0, 16), (2, 4)))
    up_weight = centred(seeds[4], (FLIGHT, D, FF), D ** -0.5, 0.09375, ((0, 16), (2, 4)))
    down_weight = centred(seeds[5], (FLIGHT, FF, D), FF ** -0.5, 0.1875, ((0, 16), (1, 4), (2, 16)))
    return dict(tokens=tokens, routes=routes, route_weights=route_weights, gate_weight=gate_weight, up_weight=up_weight, down_weight=down_weight)


def expert_rows(slot_rows, gate_mat, up_mat, down_mat):
    gate_act = jnp.dot(slot_rows, gate_mat, preferred_element_type=jnp.float32)
    up_act = jnp.dot(slot_rows, up_mat, preferred_element_type=jnp.float32)
    hidden = (jax.nn.silu(gate_act) * up_act).astype(jnp.bfloat16)
    quarter = FF // N_HEAD
    total = jnp.zeros((slot_rows.shape[0], D), jnp.float32)
    for portion in range(N_HEAD):
        partial_value = jnp.dot(hidden[:, portion * quarter:(portion + 1) * quarter], down_mat[portion * quarter:(portion + 1) * quarter], preferred_element_type=jnp.float32)
        rounded = lax.optimization_barrier(partial_value.astype(jnp.bfloat16))
        total = total + rounded.astype(jnp.float32)
    return total.astype(jnp.bfloat16)


def reference(tokens, routes, route_weights, gate_weight, up_weight, down_weight):
    blocks_count = TOKENS // TOK_DEV

    def one_expert(carry, inputs):
        number, gate_mat, up_mat, down_mat = inputs
        target = number * EXP_LOCAL
        matches = routes == target
        chosen = jnp.any(matches, axis=1)
        weight = jnp.sum(jnp.where(matches, route_weights, 0.0), axis=1)
        blocks = chosen.reshape(blocks_count, TOK_DEV).astype(jnp.int32)
        position = jnp.cumsum(blocks, axis=1) - 1
        slot_ids = jnp.arange(CAP, dtype=jnp.int32)
        match_table = (blocks[:, None, :] == 1) & (position[:, None, :] == slot_ids[None, :, None])
        member = jnp.sum(match_table.astype(jnp.int32), axis=2)
        within = jnp.sum(jnp.where(match_table, jnp.arange(TOK_DEV, dtype=jnp.int32)[None, None, :], 0), axis=2).astype(jnp.int32)
        row_index = (jnp.arange(blocks_count, dtype=jnp.int32)[:, None] * TOK_DEV + within).reshape(-1).astype(jnp.int32)
        slot_rows = jnp.where((member.reshape(-1) == 1)[:, None], tokens[row_index], jnp.zeros((), tokens.dtype))
        results = expert_rows(slot_rows, gate_mat, up_mat, down_mat)
        back_index = ((jnp.arange(TOKENS, dtype=jnp.int32) // TOK_DEV) * CAP + jnp.maximum(position.reshape(-1), 0)).astype(jnp.int32)
        contribution = jnp.where(chosen[:, None], weight[:, None] * results[back_index].astype(jnp.float32), 0.0)
        return carry + contribution, None

    start = jnp.zeros((TOKENS, D), jnp.float32)
    numbers = jnp.arange(FLIGHT, dtype=jnp.int32)
    total, _ = lax.scan(one_expert, start, (numbers, gate_weight, up_weight, down_weight))
    return total.astype(jnp.bfloat16)
```

```python
import jax
import jax.numpy as jnp
from jax import lax
from jax.experimental import pallas as pl
from jax.experimental.pallas import tpu as pltpu
from jax.sharding import PartitionSpec as P

MESH = pl.DeviceIdType.MESH
CAP = 16
NZ = 16
NY = 8
NX = 4
QUARTER = 1024
ROWS = NZ * CAP
GROUPS = ((0, 5), (5, 11), (11, 16))
Y_OFFSETS = (1, -1, 2, -2, 3, -3, 4)


def offset_of(k):
    size = 8 - (k + 1) // 2
    return size * (2 * (k % 2) - 1)


def y_index(off):
    return Y_OFFSETS.index((off + 3) % NY - 3)


def rows_of(k):
    return pl.ds(pl.multiple_of(k * CAP, CAP), CAP)


def kernel(
    tokens, routes, route_weights, gate, up, down,
    out,
    tok, rts, rtw, wg, wu, dn, outbox, arr, hid, part, relay_out, relay_in, sums_out, sums_in, summed, ret,
    load_sem, zs, zr, xs, xr, ys, yr, cs, cr, ls, lr, ss, sr, bs, br,
):
    dp = lax.axis_index("dp")
    y, core = dp // 2, dp % 2
    e = lax.axis_index("expert")
    h = lax.axis_index("head")

    def z_peer(off):
        return {"expert": (e + off + 2 * NZ) % NZ}

    def x_peer(off):
        return {"head": (h + off + NX) % NX}

    def y_dp(off):
        return ((y + off + NY) % NY) * 2 + core

    sibling = y * 2 + (1 - core)

    loads = [
        pltpu.make_async_copy(routes, rts, load_sem.at[0]),
        pltpu.make_async_copy(route_weights, rtw, load_sem.at[1]),
        pltpu.make_async_copy(
            tokens.at[:, pl.ds(pl.multiple_of(h * QUARTER, QUARTER), QUARTER)], tok, load_sem.at[2]
        ),
        pltpu.make_async_copy(down.at[0], dn.at[dp], load_sem.at[3]),
    ]
    for r, off in enumerate((0, -1, 1, 2)):
        q = (h + off + NX) % NX
        src = pl.ds(pl.multiple_of(q * QUARTER, QUARTER), QUARTER)
        loads.append(pltpu.make_async_copy(gate.at[0, src], wg.at[r], load_sem.at[4 + 2 * r]))
        loads.append(pltpu.make_async_copy(up.at[0, src], wu.at[r], load_sem.at[5 + 2 * r]))
    for copy in loads:
        copy.start()

    bar = pltpu.get_barrier_semaphore()

    def greet(i, c):
        pl.semaphore_signal(bar, inc=1, device_id=z_peer(i), device_id_type=MESH)
        return c

    lax.fori_loop(1, NZ, greet, 0)
    for off in (1, -1, 2):
        pl.semaphore_signal(bar, inc=1, device_id=x_peer(off), device_id_type=MESH)
    for off in (1, -1, 2, -2):
        pl.semaphore_signal(bar, inc=1, device_id={"dp": y_dp(off)}, device_id_type=MESH)
    pl.semaphore_signal(bar, inc=1, device_id={"dp": sibling}, device_id_type=MESH)

    tok_rows = tok.shape[0]
    col = lax.broadcasted_iota(jnp.int32, (tok_rows, ROWS), 1)
    block = col >> 4
    slot = col & (CAP - 1)
    size = 8 - ((block + 1) >> 1)
    target = ((e + NZ + jnp.where((block & 1) == 1, size, -size)) & (NZ - 1)) * 8
    loads[0].wait()
    loads[1].wait()
    chosen = jnp.zeros((tok_rows, ROWS), jnp.float32)
    weight = jnp.zeros((tok_rows, ROWS), jnp.float32)
    for i in range(8):
        match = rts[:, i : i + 1] == target
        chosen = jnp.where(match, 1.0, chosen)
        weight = jnp.where(match, rtw[:, i : i + 1], weight)
    earlier = (
        lax.broadcasted_iota(jnp.int32, (tok_rows, tok_rows), 0)
        >= lax.broadcasted_iota(jnp.int32, (tok_rows, tok_rows), 1)
    )
    count = jnp.dot(
        jnp.where(earlier, 1.0, 0.0).astype(jnp.bfloat16),
        chosen.astype(jnp.bfloat16),
        preferred_element_type=jnp.float32,
    )
    picked = jnp.where(count == (slot + 1).astype(jnp.float32), chosen, 0.0)
    mix = picked * weight
    mix_high = mix.astype(jnp.bfloat16)
    mix_low = (mix - mix_high.astype(jnp.float32)).astype(jnp.bfloat16)
    loads[2].wait()
    outbox[...] = lax.dot_general(
        picked.astype(jnp.bfloat16), tok[...], (((0,), (0,)), ((), ())), preferred_element_type=jnp.float32
    ).astype(jnp.bfloat16)
    loads[3].wait()

    pl.semaphore_wait(bar, (NZ - 1) + 3 + 4 + 1)

    def y_copy(block_off, to_off):
        there = y_index(block_off - to_off)
        return pltpu.make_async_remote_copy(
            src_ref=dn.at[y_dp(block_off)],
            dst_ref=dn.at[y_dp(block_off)],
            send_sem=ys.at[there],
            recv_sem=yr.at[there],
            device_id={"dp": y_dp(to_off)},
            device_id_type=MESH,
        )

    def y_arrived(off):
        pltpu.make_async_remote_copy(
            src_ref=dn.at[y_dp(off)],
            dst_ref=dn.at[y_dp(off)],
            send_sem=ys.at[y_index(off)],
            recv_sem=yr.at[y_index(off)],
            device_id={"dp": y_dp(off)},
            device_id_type=MESH,
        ).wait_recv()

    def core_copy(off):
        i = (off + NY) % NY
        return pltpu.make_async_remote_copy(
            src_ref=dn.at[y_dp(off)],
            dst_ref=dn.at[y_dp(off)],
            send_sem=cs.at[i],
            recv_sem=cr.at[i],
            device_id={"dp": sibling},
            device_id_type=MESH,
        )

    def core_arrived(off):
        i = (off + NY) % NY
        there = ((y + off + NY) % NY) * 2 + (1 - core)
        pltpu.make_async_remote_copy(
            src_ref=dn.at[there],
            dst_ref=dn.at[there],
            send_sem=cs.at[i],
            recv_sem=cr.at[i],
            device_id={"dp": sibling},
            device_id_type=MESH,
        ).wait_recv()

    def z_copy(k):
        return pltpu.make_async_remote_copy(
            src_ref=outbox.at[rows_of(k)],
            dst_ref=arr.at[0, rows_of(k)],
            send_sem=zs.at[k],
            recv_sem=zr.at[k],
            device_id=z_peer(offset_of(k)),
            device_id_type=MESH,
        )

    def x_copy(j, off, k):
        return pltpu.make_async_remote_copy(
            src_ref=arr.at[0, rows_of(k)],
            dst_ref=arr.at[j + 1, rows_of(k)],
            send_sem=xs.at[j, k],
            recv_sem=xr.at[j, k],
            device_id=x_peer(off),
            device_id_type=MESH,
        )

    def back_copy(k):
        return pltpu.make_async_remote_copy(
            src_ref=summed.at[rows_of(k)],
            dst_ref=ret.at[rows_of(k)],
            send_sem=bs.at[k],
            recv_sem=br.at[k],
            device_id=z_peer(-offset_of(k)),
            device_id_type=MESH,
        )

    def loop(lo, hi, step):
        def run(k, c):
            step(k)
            return c

        lax.fori_loop(lo, hi, run, 0)

    def spread(k):
        for j, off in enumerate((1, -1, 2)):
            x_copy(j, off, k).start()

    def pass_on(k):
        z_copy(k).wait_recv()
        spread(k)

    y_first = [y_copy(0, off) for off in (1, -1, 2, -2)]
    loop(0, NZ - 1, lambda k: z_copy(k).start())
    for copy in y_first:
        copy.start()
    core_copy(0).start()
    arr[0, (NZ - 1) * CAP :, :] = outbox[(NZ - 1) * CAP :, :]
    spread(NZ - 1)

    loop(0, 3, pass_on)
    y_arrived(-2)
    y_arrived(2)
    y_second = [y_copy(-2, 1), y_copy(-2, 2), y_copy(2, -1)]
    for copy in y_second:
        copy.start()
    y_arrived(-1)
    y_arrived(1)
    for off in (-1, 1, -2, 2):
        core_copy(off).start()
    for copy in loads[4:]:
        copy.wait()
    loop(3, 7, pass_on)

    def expert_front(first, last):
        n = (last - first) * CAP
        rows = slice(first * CAP, last * CAP)
        gate_act = jnp.zeros((n, wg.shape[2]), jnp.float32)
        up_act = jnp.zeros((n, wg.shape[2]), jnp.float32)
        for r in range(NX):
            if r:
                off = (1, -1, 2)[r - 1]
                loop(first, last, lambda k: x_copy(r - 1, off, k).wait_recv())
            a = arr[r, rows, :]
            gate_act += jnp.dot(a, wg[r], preferred_element_type=jnp.float32)
            up_act += jnp.dot(a, wu[r], preferred_element_type=jnp.float32)
        hidden = gate_act / (1.0 + jnp.exp(-gate_act)) * up_act
        hid[rows, :] = hidden.astype(jnp.bfloat16)

    def relay_copy(g, side):
        first, last = GROUPS[g]
        middle = (first + last) // 2
        lo, hi = (first, middle) if side == 0 else (middle, last)
        rows = pl.ds(lo * CAP, (hi - lo) * CAP)
        return pltpu.make_async_remote_copy(
            src_ref=relay_out.at[rows],
            dst_ref=relay_in.at[rows],
            send_sem=ls.at[g, side],
            recv_sem=lr.at[g, side],
            device_id=x_peer(1 - 2 * side),
            device_id_type=MESH,
        )

    def sums_copy(g, side):
        first, last = GROUPS[g]
        rows = pl.ds(first * CAP, (last - first) * CAP)
        return pltpu.make_async_remote_copy(
            src_ref=sums_out.at[side, rows],
            dst_ref=sums_in.at[side, rows],
            send_sem=ss.at[g, side],
            recv_sem=sr.at[g, side],
            device_id=x_peer(1 - 2 * side),
            device_id_type=MESH,
        )

    def expert_back(g):
        first, last = GROUPS[g]
        rows = slice(first * CAP, last * CAP)
        hidden = hid[rows, :]
        for r, off in ((3, 2), (1, 1), (2, -1), (0, 0)):
            q = (h + off + NX) % NX
            for b in range(4):
                value = jnp.dot(hidden, dn[q * 4 + b], preferred_element_type=jnp.float32)
                cols = slice(b * 256, (b + 1) * 256)
                if r == 3:
                    relay_out[rows, cols] = value.astype(jnp.bfloat16)
                else:
                    part[r, rows, cols] = value
            if r == 3:
                relay_copy(g, 0).start()
                relay_copy(g, 1).start()

    def relay(g):
        first, last = GROUPS[g]
        middle = (first + last) // 2
        for side in range(2):
            relay_copy(g, side).wait_recv()
            lo, hi = (first, middle) if side == 0 else (middle, last)
            through = slice(lo * CAP, hi * CAP)
            own = slice(middle * CAP, last * CAP) if side == 0 else slice(first * CAP, middle * CAP)
            sums_out[side, own, :] = part[1 + side, own, :].astype(jnp.bfloat16)
            sums_out[side, through, :] = (
                part[1 + side, through, :] + relay_in[through, :].astype(jnp.float32)
            ).astype(jnp.bfloat16)
            sums_copy(g, side).start()

    def finish(g):
        first, last = GROUPS[g]
        rows = slice(first * CAP, last * CAP)
        sums_copy(g, 0).wait_recv()
        sums_copy(g, 1).wait_recv()
        summed[rows, :] = (
            part[0, rows, :]
            + sums_in[0, rows, :].astype(jnp.float32)
            + sums_in[1, rows, :].astype(jnp.float32)
        ).astype(jnp.bfloat16)
        loop(first, min(last, NZ - 1), lambda k: back_copy(k).start())

    expert_front(*GROUPS[0])
    for off in (-3, 3, 4):
        y_arrived(off)
        core_copy(off).start()
    for i in range(NY):
        core_arrived(i)
    expert_back(0)
    loop(7, 11, pass_on)
    relay(0)
    loop(11, NZ - 1, pass_on)
    expert_front(*GROUPS[1])
    expert_back(1)
    finish(0)
    relay(1)
    expert_front(*GROUPS[2])
    expert_back(2)
    finish(1)
    relay(2)
    finish(2)
    ret[(NZ - 1) * CAP :, :] = summed[(NZ - 1) * CAP :, :]

    loop(0, NZ - 1, lambda k: z_copy(k).wait_send())
    for j, off in enumerate((1, -1, 2)):
        loop(0, NZ, lambda k: x_copy(j, off, k).wait_send())
    for copy in y_first + y_second:
        copy.wait_send()
    for i in range(NY):
        core_copy(i).wait_send()
    for g in range(len(GROUPS)):
        for side in range(2):
            relay_copy(g, side).wait_send()
            sums_copy(g, side).wait_send()
    loop(0, NZ - 1, lambda k: back_copy(k).wait_send())

    loop(0, NZ - 1, lambda k: back_copy(k).wait_recv())
    combined = jnp.dot(mix_high, ret[...], preferred_element_type=jnp.float32)
    combined += jnp.dot(mix_low, ret[...], preferred_element_type=jnp.float32)
    out[...] = combined.astype(jnp.bfloat16)


def body(tokens, routes, route_weights, gate_weight, up_weight, down_weight):
    tok_rows = tokens.shape[0]
    hidden = gate_weight.shape[2]
    bf16, f32 = jnp.bfloat16, jnp.float32
    dma = pltpu.SemaphoreType.DMA
    groups = len(GROUPS)
    return pl.pallas_call(
        kernel,
        out_shape=jax.ShapeDtypeStruct((tok_rows, QUARTER), bf16),
        in_specs=[pl.BlockSpec(memory_space=pl.ANY)] * 6,
        out_specs=pl.BlockSpec(memory_space=pltpu.VMEM),
        scratch_shapes=[
            pltpu.VMEM((tok_rows, QUARTER), bf16),
            pltpu.VMEM((tok_rows, 8), jnp.int32),
            pltpu.VMEM((tok_rows, 8), f32),
            pltpu.VMEM((NX, QUARTER, hidden), bf16),
            pltpu.VMEM((NX, QUARTER, hidden), bf16),
            pltpu.VMEM((2 * NY, hidden, 256), bf16),
            pltpu.VMEM((ROWS, QUARTER), bf16),
            pltpu.VMEM((NX, ROWS, QUARTER), bf16),
            pltpu.VMEM((ROWS, hidden), bf16),
            pltpu.VMEM((3, ROWS, QUARTER), f32),
            pltpu.VMEM((ROWS, QUARTER), bf16),
            pltpu.VMEM((ROWS, QUARTER), bf16),
            pltpu.VMEM((2, ROWS, QUARTER), bf16),
            pltpu.VMEM((2, ROWS, QUARTER), bf16),
            pltpu.VMEM((ROWS, QUARTER), bf16),
            pltpu.VMEM((ROWS, QUARTER), bf16),
            dma((12,)),
            dma((NZ,)), dma((NZ,)),
            dma((3, NZ)), dma((3, NZ)),
            dma((7,)), dma((7,)),
            dma((NY,)), dma((NY,)),
            dma((groups, 2)), dma((groups, 2)),
            dma((groups, 2)), dma((groups, 2)),
            dma((NZ,)), dma((NZ,)),
        ],
        compiler_params=pltpu.CompilerParams(
            collective_id=0, has_side_effects=True, vmem_limit_bytes=48 * 2**20
        ),
        cost_estimate=pl.CostEstimate(
            flops=2 * ROWS * hidden * 3 * 4096, bytes_accessed=6 * 2**20, transcendentals=ROWS * hidden
        ),
    )(tokens, routes, route_weights, gate_weight, up_weight, down_weight)


def solution(mesh):
    return jax.shard_map(
        body,
        mesh=mesh,
        in_specs=(
            P(("dp", "expert"), None),
            P(("dp", "expert"), None),
            P(("dp", "expert"), None),
            P("expert", None, "head"),
            P("expert", None, "head"),
            P("expert", "head", "dp"),
        ),
        out_specs=P(("dp", "expert"), "head"),
        check_vma=False,
    )
```

```python
import jax
import jax.numpy as jnp
from jax import lax
from jax.experimental import pallas as pl
from jax.experimental.pallas import tpu as pltpu
from jax.sharding import PartitionSpec as P

MESH = pl.DeviceIdType.MESH
CAP = 16
NZ = 16
NY = 8
NX = 4
QUARTER = 1024
ROWS = NZ * CAP
FRAG = 32
DIRECT = 13
GROUPS = ((0, 5), (5, 9), (9, 13), (13, 16))
Y_OFFSETS = (1, -1, 2, -2, 3, -3, 4)


def offset_of(k):
    return (k + 1) // 2 * (2 * (k % 2) - 1)


def y_index(off):
    return Y_OFFSETS.index((off + 3) % NY - 3)


def rows_of(k):
    return pl.ds(pl.multiple_of(k * CAP, CAP), CAP)


def kernel(
    tokens, routes, route_weights, gate, up, down,
    out,
    tok, rts, rtw, wg, wu, own_down, dn, outbox, arr, hid, summed, ret, mixing, total,
    load_sem, zs, zr, xs, xr, fs, fr, ys, yr, cs, cr, hs, hr, bs, br,
):
    dp = lax.axis_index("dp")
    y, core = dp // 2, dp % 2
    e = lax.axis_index("expert")
    h = lax.axis_index("head")

    def z_peer(off):
        return {"expert": (e + off + 2 * NZ) % NZ}

    def x_peer(off):
        return {"head": (h + off + NX) % NX}

    def y_at(off):
        return (y + off + NY) % NY

    def y_dp(off):
        return y_at(off) * 2 + core

    sibling = y * 2 + (1 - core)

    loads = [
        pltpu.make_async_copy(routes, rts, load_sem.at[0]),
        pltpu.make_async_copy(route_weights, rtw, load_sem.at[1]),
        pltpu.make_async_copy(
            tokens.at[:, pl.ds(pl.multiple_of(h * QUARTER, QUARTER), QUARTER)], tok, load_sem.at[2]
        ),
        pltpu.make_async_copy(down.at[0], own_down, load_sem.at[3]),
    ]
    for r, off in enumerate((0, -1, 1, 2)):
        q = (h + off + NX) % NX
        src = pl.ds(pl.multiple_of(q * QUARTER, QUARTER), QUARTER)
        loads.append(pltpu.make_async_copy(gate.at[0, src], wg.at[r], load_sem.at[4 + 2 * r]))
        loads.append(pltpu.make_async_copy(up.at[0, src], wu.at[r], load_sem.at[5 + 2 * r]))
    for copy in loads:
        copy.start()

    bar = pltpu.get_barrier_semaphore()

    def greet(i, c):
        pl.semaphore_signal(bar, inc=1, device_id=z_peer(i), device_id_type=MESH)
        return c

    lax.fori_loop(1, NZ, greet, 0)
    for off in (1, -1, 2):
        pl.semaphore_signal(bar, inc=1, device_id=x_peer(off), device_id_type=MESH)
    for off in (1, -1, 2, -2):
        pl.semaphore_signal(bar, inc=1, device_id={"dp": y_dp(off)}, device_id_type=MESH)
    pl.semaphore_signal(bar, inc=1, device_id={"dp": sibling}, device_id_type=MESH)
    column = y // 2
    at_home = (column == h).astype(jnp.int32)
    for s in range(2):
        for p in range(NX):
            @pl.when((y != 2 * h + s) | (h != p))
            def _():
                pl.semaphore_signal(
                    bar, inc=1, device_id={"dp": (2 * h + s) * 2 + core, "head": p}, device_id_type=MESH
                )

    tok_rows = tok.shape[0]
    row = lax.broadcasted_iota(jnp.int32, (ROWS, tok_rows), 0)
    block = row >> 4
    slot = row & (CAP - 1)
    size = (block + 1) >> 1
    target = ((e + NZ + jnp.where((block & 1) == 1, size, -size)) & (NZ - 1)) * 8
    loads[0].wait()
    loads[1].wait()
    chosen = jnp.zeros((ROWS, tok_rows), jnp.float32)
    weight = jnp.zeros((ROWS, tok_rows), jnp.float32)
    for i in range(8):
        match = rts[i : i + 1, :] == target
        chosen = jnp.where(match, 1.0, chosen)
        weight = jnp.where(match, rtw[i : i + 1, :], weight)
    upto = (
        lax.broadcasted_iota(jnp.int32, (tok_rows, tok_rows), 0)
        <= lax.broadcasted_iota(jnp.int32, (tok_rows, tok_rows), 1)
    )
    count = jnp.dot(
        chosen.astype(jnp.bfloat16),
        jnp.where(upto, 1.0, 0.0).astype(jnp.bfloat16),
        preferred_element_type=jnp.float32,
    )
    picked = jnp.where(count == (slot + 1).astype(jnp.float32), chosen, 0.0)
    loads[2].wait()
    outbox[...] = jnp.dot(
        picked.astype(jnp.bfloat16), tok[...], preferred_element_type=jnp.float32
    ).astype(jnp.bfloat16)
    loads[3].wait()

    pl.semaphore_wait(bar, (NZ - 1) + 3 + 4 + 1 + NY - at_home)

    def frag_copy(i):
        return pltpu.make_async_remote_copy(
            src_ref=own_down.at[pl.ds(i * FRAG, FRAG)],
            dst_ref=dn.at[core, i, y % 2, h],
            send_sem=fs.at[i],
            recv_sem=fr.at[y % 2, h],
            device_id={"dp": i * 2 + core, "head": column},
            device_id_type=MESH,
        )

    def frag_arrived(s, p):
        pltpu.make_async_remote_copy(
            src_ref=own_down.at[pl.ds(0, FRAG)],
            dst_ref=dn.at[core, y, s, p],
            send_sem=fs.at[0],
            recv_sem=fr.at[s, p],
            device_id={"dp": (2 * h + s) * 2 + core, "head": p},
            device_id_type=MESH,
        ).wait_recv()

    def own_frag():
        return pltpu.make_async_copy(
            own_down.at[pl.ds(pl.multiple_of(y * FRAG, FRAG), FRAG)], dn.at[core, y, y % 2, h], load_sem.at[3]
        )

    def y_copy(block_off, to_off):
        there = y_index(block_off - to_off)
        return pltpu.make_async_remote_copy(
            src_ref=dn.at[core, y_at(block_off)],
            dst_ref=dn.at[core, y_at(block_off)],
            send_sem=ys.at[there],
            recv_sem=yr.at[there],
            device_id={"dp": y_dp(to_off)},
            device_id_type=MESH,
        )

    def y_arrived(off):
        pltpu.make_async_remote_copy(
            src_ref=dn.at[core, y_at(off)],
            dst_ref=dn.at[core, y_at(off)],
            send_sem=ys.at[y_index(off)],
            recv_sem=yr.at[y_index(off)],
            device_id={"dp": y_dp(1)},
            device_id_type=MESH,
        ).wait_recv()

    def core_copy(off):
        i = (off + NY) % NY
        return pltpu.make_async_remote_copy(
            src_ref=dn.at[core, y_at(off)],
            dst_ref=dn.at[core, y_at(off)],
            send_sem=cs.at[i],
            recv_sem=cr.at[i],
            device_id={"dp": sibling},
            device_id_type=MESH,
        )

    def core_arrived(off):
        i = (off + NY) % NY
        pltpu.make_async_remote_copy(
            src_ref=dn.at[1 - core, y_at(off)],
            dst_ref=dn.at[1 - core, y_at(off)],
            send_sem=cs.at[i],
            recv_sem=cr.at[i],
            device_id={"dp": sibling},
            device_id_type=MESH,
        ).wait_recv()

    def z_copy(k):
        return pltpu.make_async_remote_copy(
            src_ref=outbox.at[rows_of(k)],
            dst_ref=arr.at[0, rows_of(k)],
            send_sem=zs.at[k],
            recv_sem=zr.at[k],
            device_id=z_peer(offset_of(k)),
            device_id_type=MESH,
        )

    def x_copy(j, k):
        return pltpu.make_async_remote_copy(
            src_ref=arr.at[0, rows_of(k)],
            dst_ref=arr.at[j + 1, rows_of(k)],
            send_sem=xs.at[j, k],
            recv_sem=xr.at[j, k],
            device_id=x_peer(1 - 2 * j),
            device_id_type=MESH,
        )

    def far_copy(k):
        j = k % 2
        return pltpu.make_async_remote_copy(
            src_ref=arr.at[j + 1, rows_of(k)],
            dst_ref=arr.at[3, rows_of(k)],
            send_sem=xs.at[2, k],
            recv_sem=xr.at[2, k],
            device_id=x_peer(1 - 2 * j),
            device_id_type=MESH,
        )

    def back_copy(k):
        return pltpu.make_async_remote_copy(
            src_ref=summed.at[rows_of(k)],
            dst_ref=ret.at[rows_of(k)],
            send_sem=bs.at[k],
            recv_sem=br.at[k],
            device_id=z_peer(-offset_of(k)),
            device_id_type=MESH,
        )

    def loop(lo, hi, step):
        def run(k, c):
            step(k)
            return c

        lax.fori_loop(lo, hi, run, 0)

    def direct_copy(k):
        return pltpu.make_async_remote_copy(
            src_ref=arr.at[0, rows_of(k)],
            dst_ref=arr.at[3, rows_of(k)],
            send_sem=xs.at[2, k],
            recv_sem=xr.at[2, k],
            device_id=x_peer(2),
            device_id_type=MESH,
        )

    def spread(k):
        x_copy(0, k).start()
        x_copy(1, k).start()

    def forward(k):
        x_copy(k % 2, k).wait_recv()
        far_copy(k).start()

    def pass_on(k):
        z_copy(k).wait_recv()
        spread(k)

    for i in range(NY):
        @pl.when((column != h) | (y != i))
        def _():
            frag_copy(i).start()

    @pl.when(column == h)
    def _():
        own_frag().start()

    loop(1, NZ, lambda k: z_copy(k).start())
    arr[0, :CAP, :] = outbox[:CAP, :]
    spread(0)

    mix = (picked * weight).T
    mix_high = mix.astype(jnp.bfloat16)
    mixing[0] = mix_high
    mixing[1] = (mix - mix_high.astype(jnp.float32)).astype(jnp.bfloat16)

    def expert_front(g):
        first, last = GROUPS[g]
        n = (last - first) * CAP
        rows = slice(first * CAP, last * CAP)
        gate_act = jnp.zeros((n, wg.shape[2]), jnp.float32)
        up_act = jnp.zeros((n, wg.shape[2]), jnp.float32)
        for r in range(NX):
            if r == 1:
                loop(first, last, lambda k: x_copy(1 - k % 2, k).wait_recv())
                loop(max(first, DIRECT), last, lambda k: x_copy(k % 2, k).wait_recv())
            if r == 3:
                loop(first, last, lambda k: far_copy(k).wait_recv())
            a = arr[r, rows, :]
            gate_act += jnp.dot(a, wg[r], preferred_element_type=jnp.float32)
            up_act += jnp.dot(a, wu[r], preferred_element_type=jnp.float32)
        hidden = gate_act / (1.0 + jnp.exp(-gate_act)) * up_act
        hid[h, rows, :] = hidden.astype(jnp.bfloat16)
        for j in range(3):
            hid_copy(g, j).start()

    def hid_copy(g, j):
        first, last = GROUPS[g]
        rows = pl.ds(first * CAP, (last - first) * CAP)
        return pltpu.make_async_remote_copy(
            src_ref=hid.at[h, rows],
            dst_ref=hid.at[h, rows],
            send_sem=hs.at[g, j],
            recv_sem=hr.at[g, j],
            device_id=x_peer((1, -1, 2)[j]),
            device_id_type=MESH,
        )

    def hid_arrived(g, j):
        first, last = GROUPS[g]
        rows = pl.ds(first * CAP, (last - first) * CAP)
        off = (1, -1, 2)[j]
        source = (h - off + NX) % NX
        pltpu.make_async_remote_copy(
            src_ref=hid.at[source, rows],
            dst_ref=hid.at[source, rows],
            send_sem=hs.at[g, j],
            recv_sem=hr.at[g, j],
            device_id=x_peer(off),
            device_id_type=MESH,
        ).wait_recv()

    def expert_back(g):
        first, last = GROUPS[g]
        rows = slice(first * CAP, last * CAP)
        for j in range(3):
            hid_arrived(g, j)
        for s in range(2):
            for c in range(2):
                value = sum(
                    jnp.dot(
                        hid[p, rows, :],
                        dn[c, :, s, p].reshape(NY * FRAG, dn.shape[-1]),
                        preferred_element_type=jnp.float32,
                    )
                    for p in range(NX)
                )
                b = 2 * s + c
                summed[rows, b * 256 : (b + 1) * 256] = value.astype(jnp.bfloat16)
        loop(max(first, 1), last, lambda k: back_copy(k).start())

    def pass_far(k):
        pass_on(k)
        direct_copy(k).start()

    loop(1, 3, pass_on)
    for s in range(2):
        for p in range(NX):
            @pl.when((y != 2 * h + s) | (h != p))
            def _():
                frag_arrived(s, p)

    @pl.when(column == h)
    def _():
        own_frag().wait()

    y_first = [y_copy(0, off) for off in (2, -2, 1, -1)]
    for copy in y_first:
        copy.start()
    core_copy(0).start()
    loop(3, 5, pass_on)
    forward(0)
    loop(5, 7, pass_on)
    loop(1, 3, forward)
    for copy in loads[4:]:
        copy.wait()
    loop(7, 9, pass_on)
    loop(3, 5, forward)
    loop(9, 11, pass_on)
    loop(5, 7, forward)
    expert_front(0)
    y_arrived(-2)
    y_arrived(2)
    y_second = [y_copy(-2, 2), y_copy(-2, 1), y_copy(2, -1)]
    for copy in y_second:
        copy.start()
    loop(11, 13, pass_on)
    loop(7, 9, forward)
    y_arrived(-1)
    y_arrived(1)
    for off in (-1, 1, -2, 2):
        core_copy(off).start()
    loop(13, 15, pass_far)
    loop(9, 11, forward)
    expert_front(1)
    loop(11, 13, forward)
    pass_far(15)
    expert_front(2)
    for off in (-3, 3, 4):
        y_arrived(off)
        core_copy(off).start()
    expert_front(3)
    for i in range(NY):
        core_arrived(i)
    expert_back(2)
    expert_back(3)
    expert_back(1)
    expert_back(0)
    ret[:CAP, :] = summed[:CAP, :]

    for i in range(NY):
        @pl.when((column != h) | (y != i))
        def _():
            frag_copy(i).wait_send()
    loop(1, NZ, lambda k: z_copy(k).wait_send())
    for j in range(2):
        loop(0, NZ, lambda k: x_copy(j, k).wait_send())
    loop(0, DIRECT, lambda k: far_copy(k).wait_send())
    loop(DIRECT, NZ, lambda k: direct_copy(k).wait_send())
    for copy in y_first + y_second:
        copy.wait_send()
    for i in range(NY):
        core_copy(i).wait_send()
    for g in range(len(GROUPS)):
        for j in range(3):
            hid_copy(g, j).wait_send()

    def mixed(lo, hi):
        rows = slice(lo * CAP, hi * CAP)
        return sum(
            jnp.dot(mixing[i, :, rows], ret[rows, :], preferred_element_type=jnp.float32) for i in range(2)
        )

    half = NZ // 2
    loop(half, NZ, lambda k: back_copy(k).wait_recv())
    total[...] = mixed(half, NZ)
    loop(1, half, lambda k: back_copy(k).wait_recv())
    out[...] = (total[...] + mixed(0, half)).astype(jnp.bfloat16)
    loop(1, NZ, lambda k: back_copy(k).wait_send())


def body(tokens, routes, route_weights, gate_weight, up_weight, down_weight):
    tok_rows = tokens.shape[0]
    hidden = gate_weight.shape[2]
    bf16, f32 = jnp.bfloat16, jnp.float32
    dma = pltpu.SemaphoreType.DMA
    groups = len(GROUPS)
    return pl.pallas_call(
        kernel,
        out_shape=jax.ShapeDtypeStruct((tok_rows, QUARTER), bf16),
        in_specs=[pl.BlockSpec(memory_space=pltpu.HBM)] * 6,
        out_specs=pl.BlockSpec(memory_space=pltpu.VMEM),
        scratch_shapes=[
            pltpu.VMEM((tok_rows, QUARTER), bf16),
            pltpu.VMEM((8, tok_rows), jnp.int32),
            pltpu.VMEM((8, tok_rows), f32),
            pltpu.VMEM((NX, QUARTER, hidden), bf16),
            pltpu.VMEM((NX, QUARTER, hidden), bf16),
            pltpu.VMEM((hidden, 256), bf16),
            pltpu.VMEM((2, NY, 2, NX, FRAG, 256), bf16),
            pltpu.VMEM((ROWS, QUARTER), bf16),
            pltpu.VMEM((NX, ROWS, QUARTER), bf16),
            pltpu.VMEM((NX, ROWS, hidden), bf16),
            pltpu.VMEM((ROWS, QUARTER), bf16),
            pltpu.VMEM((ROWS, QUARTER), bf16),
            pltpu.VMEM((2, tok_rows, ROWS), bf16),
            pltpu.VMEM((tok_rows, QUARTER), f32),
            dma((12,)),
            dma((NZ,)), dma((NZ,)),
            dma((3, NZ)), dma((3, NZ)),
            dma((NY,)), dma((2, NX)),
            dma((7,)), dma((7,)),
            dma((NY,)), dma((NY,)),
            dma((groups, 3)), dma((groups, 3)),
            dma((NZ,)), dma((NZ,)),
        ],
        compiler_params=pltpu.CompilerParams(
            collective_id=0, has_side_effects=True, vmem_limit_bytes=62 * 2**20
        ),
        cost_estimate=pl.CostEstimate(
            flops=2 * ROWS * hidden * 3 * 4096, bytes_accessed=6 * 2**20, transcendentals=ROWS * hidden
        ),
    )(tokens, routes.T, route_weights.T, gate_weight, up_weight, down_weight)


def solution(mesh):
    return jax.shard_map(
        body,
        mesh=mesh,
        in_specs=(
            P(("dp", "expert"), None),
            P(("dp", "expert"), None),
            P(("dp", "expert"), None),
            P("expert", None, "head"),
            P("expert", None, "head"),
            P("expert", "head", "dp"),
        ),
        out_specs=P(("dp", "expert"), "head"),
        check_vma=False,
    )
```

```python
import jax
import jax.numpy as jnp
from jax import lax
from jax.experimental import pallas as pl
from jax.experimental.pallas import tpu as pltpu
from jax.sharding import PartitionSpec as P

MESH = pl.DeviceIdType.MESH
CAP = 16
NZ = 16
NY = 8
NX = 4
QUARTER = 1024
ROWS = NZ * CAP
FRAG = 32
GROUPS = ((0, 5), (5, 11), (11, 16))
Y_OFFSETS = (1, -1, 2, -2, 3, -3, 4)


def offset_of(k):
    return (8 - (k + 1) // 2) * (2 * (k % 2) - 1)


def y_index(off):
    return Y_OFFSETS.index((off + 3) % NY - 3)


def rows_of(k):
    return pl.ds(pl.multiple_of(k * CAP, CAP), CAP)


def kernel(
    tokens, routes, route_weights, gate, up, down,
    out,
    tok, rts, rtw, wg, wu, own_down, dn, outbox, arr, hid, summed, ret, mixing, total,
    load_sem, zs, zr, xs, xr, fs, fr, ys, yr, cs, cr, hs, hr, bs, br,
):
    dp = lax.axis_index("dp")
    y, core = dp // 2, dp % 2
    e = lax.axis_index("expert")
    h = lax.axis_index("head")

    def z_peer(off):
        return {"expert": (e + off + 2 * NZ) % NZ}

    def x_peer(off):
        return {"head": (h + off + NX) % NX}

    def y_at(off):
        return (y + off + NY) % NY

    def y_dp(off):
        return y_at(off) * 2 + core

    sibling = y * 2 + (1 - core)

    loads = [
        pltpu.make_async_copy(routes, rts, load_sem.at[0]),
        pltpu.make_async_copy(route_weights, rtw, load_sem.at[1]),
        pltpu.make_async_copy(
            tokens.at[:, pl.ds(pl.multiple_of(h * QUARTER, QUARTER), QUARTER)], tok, load_sem.at[2]
        ),
        pltpu.make_async_copy(down.at[0], own_down, load_sem.at[3]),
    ]
    for r, off in enumerate((0, -1, 1, 2)):
        q = (h + off + NX) % NX
        src = pl.ds(pl.multiple_of(q * QUARTER, QUARTER), QUARTER)
        loads.append(pltpu.make_async_copy(gate.at[0, src], wg.at[r], load_sem.at[4 + 2 * r]))
        loads.append(pltpu.make_async_copy(up.at[0, src], wu.at[r], load_sem.at[5 + 2 * r]))
    bar = pltpu.get_barrier_semaphore()

    def greet(i, c):
        pl.semaphore_signal(bar, inc=1, device_id=z_peer(i), device_id_type=MESH)
        return c

    lax.fori_loop(1, NZ, greet, 0)
    for off in (1, -1, 2):
        pl.semaphore_signal(bar, inc=1, device_id=x_peer(off), device_id_type=MESH)
    for off in (1, -1, 2, -2):
        pl.semaphore_signal(bar, inc=1, device_id={"dp": y_dp(off)}, device_id_type=MESH)
    pl.semaphore_signal(bar, inc=1, device_id={"dp": sibling}, device_id_type=MESH)
    column = y // 2
    at_home = (column == h).astype(jnp.int32)
    for s in range(2):
        for p in range(NX):
            @pl.when((y != 2 * h + s) | (h != p))
            def _():
                pl.semaphore_signal(
                    bar, inc=1, device_id={"dp": (2 * h + s) * 2 + core, "head": p}, device_id_type=MESH
                )

    for copy in loads:
        copy.start()

    tok_rows = tok.shape[0]
    row = lax.broadcasted_iota(jnp.int32, (ROWS, tok_rows), 0)
    block = row >> 4
    slot = row & (CAP - 1)
    size = 8 - ((block + 1) >> 1)
    target = ((e + NZ + jnp.where((block & 1) == 1, size, -size)) & (NZ - 1)) * 8
    loads[0].wait()
    loads[1].wait()
    chosen = jnp.zeros((ROWS, tok_rows), jnp.float32)
    weight = jnp.zeros((ROWS, tok_rows), jnp.float32)
    for i in range(8):
        match = rts[i : i + 1, :] == target
        chosen = jnp.where(match, 1.0, chosen)
        weight = jnp.where(match, rtw[i : i + 1, :], weight)
    upto = (
        lax.broadcasted_iota(jnp.int32, (tok_rows, tok_rows), 0)
        <= lax.broadcasted_iota(jnp.int32, (tok_rows, tok_rows), 1)
    )
    count = jnp.dot(
        chosen.astype(jnp.bfloat16),
        jnp.where(upto, 1.0, 0.0).astype(jnp.bfloat16),
        preferred_element_type=jnp.float32,
    )
    picked = jnp.where(count == (slot + 1).astype(jnp.float32), chosen, 0.0)
    loads[2].wait()
    outbox[...] = jnp.dot(
        picked.astype(jnp.bfloat16), tok[...], preferred_element_type=jnp.float32
    ).astype(jnp.bfloat16)
    loads[3].wait()

    pl.semaphore_wait(bar, (NZ - 1) + 3 + 4 + 1 + NY - at_home)

    def frag_copy(i):
        return pltpu.make_async_remote_copy(
            src_ref=own_down.at[pl.ds(i * FRAG, FRAG)],
            dst_ref=dn.at[core, i, y % 2, h],
            send_sem=fs.at[i],
            recv_sem=fr.at[y % 2, h],
            device_id={"dp": i * 2 + core, "head": column},
            device_id_type=MESH,
        )

    def frag_arrived(s, p):
        pltpu.make_async_remote_copy(
            src_ref=own_down.at[pl.ds(0, FRAG)],
            dst_ref=dn.at[core, y, s, p],
            send_sem=fs.at[0],
            recv_sem=fr.at[s, p],
            device_id={"dp": (2 * h + s) * 2 + core, "head": p},
            device_id_type=MESH,
        ).wait_recv()

    def own_frag():
        return pltpu.make_async_copy(
            own_down.at[pl.ds(pl.multiple_of(y * FRAG, FRAG), FRAG)], dn.at[core, y, y % 2, h], load_sem.at[3]
        )

    def y_copy(block_off, to_off):
        there = y_index(block_off - to_off)
        return pltpu.make_async_remote_copy(
            src_ref=dn.at[core, y_at(block_off)],
            dst_ref=dn.at[core, y_at(block_off)],
            send_sem=ys.at[there],
            recv_sem=yr.at[there],
            device_id={"dp": y_dp(to_off)},
            device_id_type=MESH,
        )

    def y_arrived(off):
        pltpu.make_async_remote_copy(
            src_ref=dn.at[core, y_at(off)],
            dst_ref=dn.at[core, y_at(off)],
            send_sem=ys.at[y_index(off)],
            recv_sem=yr.at[y_index(off)],
            device_id={"dp": y_dp(1)},
            device_id_type=MESH,
        ).wait_recv()

    def core_copy(off):
        i = (off + NY) % NY
        return pltpu.make_async_remote_copy(
            src_ref=dn.at[core, y_at(off)],
            dst_ref=dn.at[core, y_at(off)],
            send_sem=cs.at[i],
            recv_sem=cr.at[i],
            device_id={"dp": sibling},
            device_id_type=MESH,
        )

    def core_arrived(off):
        i = (off + NY) % NY
        pltpu.make_async_remote_copy(
            src_ref=dn.at[1 - core, y_at(off)],
            dst_ref=dn.at[1 - core, y_at(off)],
            send_sem=cs.at[i],
            recv_sem=cr.at[i],
            device_id={"dp": sibling},
            device_id_type=MESH,
        ).wait_recv()

    def z_copy(k):
        return pltpu.make_async_remote_copy(
            src_ref=outbox.at[rows_of(k)],
            dst_ref=arr.at[0, rows_of(k)],
            send_sem=zs.at[k],
            recv_sem=zr.at[k],
            device_id=z_peer(offset_of(k)),
            device_id_type=MESH,
        )

    def x_copy(j, k):
        return pltpu.make_async_remote_copy(
            src_ref=arr.at[0, rows_of(k)],
            dst_ref=arr.at[j + 1, rows_of(k)],
            send_sem=xs.at[j, k],
            recv_sem=xr.at[j, k],
            device_id=x_peer((1, -1, 2)[j]),
            device_id_type=MESH,
        )

    def back_copy(k):
        return pltpu.make_async_remote_copy(
            src_ref=summed.at[rows_of(k)],
            dst_ref=ret.at[rows_of(k)],
            send_sem=bs.at[k],
            recv_sem=br.at[k],
            device_id=z_peer(-offset_of(k)),
            device_id_type=MESH,
        )

    def loop(lo, hi, step):
        def run(k, c):
            step(k)
            return c

        lax.fori_loop(lo, hi, run, 0)

    def spread(k):
        for j in range(3):
            x_copy(j, k).start()

    def pass_on(k):
        z_copy(k).wait_recv()
        spread(k)

    for i in range(NY):
        @pl.when((column != h) | (y != i))
        def _():
            frag_copy(i).start()

    @pl.when(column == h)
    def _():
        own_frag().start()

    loop(0, NZ - 1, lambda k: z_copy(k).start())
    arr[0, -CAP:, :] = outbox[-CAP:, :]
    spread(NZ - 1)

    mix = (picked * weight).T
    mix_high = mix.astype(jnp.bfloat16)
    mixing[0] = mix_high
    mixing[1] = (mix - mix_high.astype(jnp.float32)).astype(jnp.bfloat16)

    def expert_front(g):
        first, last = GROUPS[g]
        n = (last - first) * CAP
        rows = slice(first * CAP, last * CAP)
        gate_act = jnp.zeros((n, wg.shape[2]), jnp.float32)
        up_act = jnp.zeros((n, wg.shape[2]), jnp.float32)
        for r in range(NX):
            if r:
                loop(first, last, lambda k: x_copy(r - 1, k).wait_recv())
            a = arr[r, rows, :]
            gate_act += jnp.dot(a, wg[r], preferred_element_type=jnp.float32)
            up_act += jnp.dot(a, wu[r], preferred_element_type=jnp.float32)
        hidden = gate_act / (1.0 + jnp.exp(-gate_act)) * up_act
        hid[h, rows, :] = hidden.astype(jnp.bfloat16)
        for j in range(3):
            hid_copy(g, j).start()

    def hid_copy(g, j):
        first, last = GROUPS[g]
        rows = pl.ds(first * CAP, (last - first) * CAP)
        return pltpu.make_async_remote_copy(
            src_ref=hid.at[h, rows],
            dst_ref=hid.at[h, rows],
            send_sem=hs.at[g, j],
            recv_sem=hr.at[g, j],
            device_id=x_peer((1, -1, 2)[j]),
            device_id_type=MESH,
        )

    def hid_arrived(g, j):
        first, last = GROUPS[g]
        rows = pl.ds(first * CAP, (last - first) * CAP)
        off = (1, -1, 2)[j]
        source = (h - off + NX) % NX
        pltpu.make_async_remote_copy(
            src_ref=hid.at[source, rows],
            dst_ref=hid.at[source, rows],
            send_sem=hs.at[g, j],
            recv_sem=hr.at[g, j],
            device_id=x_peer(off),
            device_id_type=MESH,
        ).wait_recv()

    def expert_back(groups):
        first, last = GROUPS[groups[0]][0], GROUPS[groups[-1]][1]
        rows = slice(first * CAP, last * CAP)
        for g in groups:
            for j in range(3):
                hid_arrived(g, j)
        for s in range(2):
            for c in range(2):
                value = sum(
                    jnp.dot(
                        hid[p, rows, :],
                        dn[c, :, s, p].reshape(NY * FRAG, dn.shape[-1]),
                        preferred_element_type=jnp.float32,
                    )
                    for p in range(NX)
                )
                b = 2 * s + c
                summed[rows, b * 256 : (b + 1) * 256] = value.astype(jnp.bfloat16)
        loop(first, min(last, NZ - 1), lambda k: back_copy(k).start())

    for s in range(2):
        for p in range(NX):
            @pl.when((y != 2 * h + s) | (h != p))
            def _():
                frag_arrived(s, p)

    @pl.when(column == h)
    def _():
        own_frag().wait()

    y_first = [y_copy(0, off) for off in (2, -2, 1, -1)]
    for copy in y_first:
        copy.start()
    core_copy(0).start()
    for copy in loads[4:]:
        copy.wait()
    loop(0, 3, pass_on)
    y_arrived(-2)
    y_arrived(2)
    y_second = [y_copy(-2, 2), y_copy(-2, 1), y_copy(2, -1)]
    for copy in y_second:
        copy.start()
    loop(3, 5, pass_on)
    y_arrived(-1)
    y_arrived(1)
    for off in (-1, 1, -2, 2):
        core_copy(off).start()
    loop(5, 7, pass_on)
    expert_front(0)
    for off in (-3, 3, 4):
        y_arrived(off)
        core_copy(off).start()
    loop(7, 11, pass_on)
    for i in range(NY):
        core_arrived(i)
    expert_back((0,))
    expert_front(1)
    loop(11, NZ - 1, pass_on)
    expert_back((1,))
    expert_front(2)
    expert_back((2,))
    ret[-CAP:, :] = summed[-CAP:, :]

    for i in range(NY):
        @pl.when((column != h) | (y != i))
        def _():
            frag_copy(i).wait_send()
    loop(0, NZ - 1, lambda k: z_copy(k).wait_send())
    for j in range(3):
        loop(0, NZ, lambda k: x_copy(j, k).wait_send())
    for copy in y_first + y_second:
        copy.wait_send()
    for i in range(NY):
        core_copy(i).wait_send()
    for g in range(len(GROUPS)):
        for j in range(3):
            hid_copy(g, j).wait_send()

    def mixed(lo, hi):
        rows = slice(lo * CAP, hi * CAP)
        return sum(
            jnp.dot(mixing[i, :, rows], ret[rows, :], preferred_element_type=jnp.float32) for i in range(2)
        )

    half = NZ // 2
    loop(0, half, lambda k: back_copy(k).wait_recv())
    total[...] = mixed(0, half)
    loop(half, NZ - 1, lambda k: back_copy(k).wait_recv())
    out[...] = (total[...] + mixed(half, NZ)).astype(jnp.bfloat16)
    loop(0, NZ - 1, lambda k: back_copy(k).wait_send())


def body(tokens, routes, route_weights, gate_weight, up_weight, down_weight):
    tok_rows = tokens.shape[0]
    hidden = gate_weight.shape[2]
    bf16, f32 = jnp.bfloat16, jnp.float32
    dma = pltpu.SemaphoreType.DMA
    groups = len(GROUPS)
    return pl.pallas_call(
        kernel,
        out_shape=jax.ShapeDtypeStruct((tok_rows, QUARTER), bf16),
        in_specs=[pl.BlockSpec(memory_space=pltpu.HBM)] * 6,
        out_specs=pl.BlockSpec(memory_space=pltpu.VMEM),
        scratch_shapes=[
            pltpu.VMEM((tok_rows, QUARTER), bf16),
            pltpu.VMEM((8, tok_rows), jnp.int32),
            pltpu.VMEM((8, tok_rows), f32),
            pltpu.VMEM((NX, QUARTER, hidden), bf16),
            pltpu.VMEM((NX, QUARTER, hidden), bf16),
            pltpu.VMEM((hidden, 256), bf16),
            pltpu.VMEM((2, NY, 2, NX, FRAG, 256), bf16),
            pltpu.VMEM((ROWS, QUARTER), bf16),
            pltpu.VMEM((NX, ROWS, QUARTER), bf16),
            pltpu.VMEM((NX, ROWS, hidden), bf16),
            pltpu.VMEM((ROWS, QUARTER), bf16),
            pltpu.VMEM((ROWS, QUARTER), bf16),
            pltpu.VMEM((2, tok_rows, ROWS), bf16),
            pltpu.VMEM((tok_rows, QUARTER), f32),
            dma((12,)),
            dma((NZ,)), dma((NZ,)),
            dma((3, NZ)), dma((3, NZ)),
            dma((NY,)), dma((2, NX)),
            dma((7,)), dma((7,)),
            dma((NY,)), dma((NY,)),
            dma((groups, 3)), dma((groups, 3)),
            dma((NZ,)), dma((NZ,)),
        ],
        compiler_params=pltpu.CompilerParams(
            collective_id=0, has_side_effects=True, vmem_limit_bytes=62 * 2**20
        ),
        cost_estimate=pl.CostEstimate(
            flops=2 * ROWS * hidden * 3 * 4096, bytes_accessed=6 * 2**20, transcendentals=ROWS * hidden
        ),
    )(tokens, routes.T, route_weights.T, gate_weight, up_weight, down_weight)


def solution(mesh):
    return jax.shard_map(
        body,
        mesh=mesh,
        in_specs=(
            P(("dp", "expert"), None),
            P(("dp", "expert"), None),
            P(("dp", "expert"), None),
            P("expert", None, "head"),
            P("expert", None, "head"),
            P("expert", "head", "dp"),
        ),
        out_specs=P(("dp", "expert"), "head"),
        check_vma=False,
    )
```

```python
import jax
import jax.numpy as jnp
from jax import lax
from jax.experimental import pallas as pl
from jax.experimental.pallas import tpu as pltpu
from jax.sharding import PartitionSpec as P

MESH = pl.DeviceIdType.MESH
CAP = 16
NZ = 16
NY = 8
NX = 4
QUARTER = 1024
ROWS = NZ * CAP
FRAG = 32
EARLY = 13
GROUPS = ((0, 5), (5, 11), (11, 16))
Y_OFFSETS = (1, -1, 2, -2, 3, -3, 4)


def offset_of(k):
    return (8 - (k + 1) // 2) * (2 * (k % 2) - 1)


def y_index(off):
    return Y_OFFSETS.index((off + 3) % NY - 3)


def rows_of(k):
    return pl.ds(pl.multiple_of(k * CAP, CAP), CAP)


def kernel(
    tokens, routes, route_weights, gate, up, down,
    out,
    tok, rts, rtw, wg, wu, own_down, dn, outbox, arr, hid, summed, ret, mixing, total,
    load_sem, zs, zr, xs, xr, fs, fr, ys, yr, cs, cr, hs, hr, bs, br,
):
    dp = lax.axis_index("dp")
    y, core = dp // 2, dp % 2
    e = lax.axis_index("expert")
    h = lax.axis_index("head")

    def z_peer(off):
        return {"expert": (e + off + 2 * NZ) % NZ}

    def x_peer(off):
        return {"head": (h + off + NX) % NX}

    def y_at(off):
        return (y + off + NY) % NY

    def y_dp(off):
        return y_at(off) * 2 + core

    sibling = y * 2 + (1 - core)

    loads = [
        pltpu.make_async_copy(routes, rts, load_sem.at[0]),
        pltpu.make_async_copy(route_weights, rtw, load_sem.at[1]),
        pltpu.make_async_copy(
            tokens.at[:, pl.ds(pl.multiple_of(h * QUARTER, QUARTER), QUARTER)], tok, load_sem.at[2]
        ),
        pltpu.make_async_copy(down.at[0], own_down, load_sem.at[3]),
    ]
    for r, off in enumerate((0, -1, 1, 2)):
        q = (h + off + NX) % NX
        src = pl.ds(pl.multiple_of(q * QUARTER, QUARTER), QUARTER)
        loads.append(pltpu.make_async_copy(gate.at[0, src], wg.at[r], load_sem.at[4 + 2 * r]))
        loads.append(pltpu.make_async_copy(up.at[0, src], wu.at[r], load_sem.at[5 + 2 * r]))
    bar = pltpu.get_barrier_semaphore()

    def greet(i, c):
        pl.semaphore_signal(bar, inc=1, device_id=z_peer(i), device_id_type=MESH)
        return c

    lax.fori_loop(1, NZ, greet, 0)
    for off in (1, -1, 2):
        pl.semaphore_signal(bar, inc=1, device_id=x_peer(off), device_id_type=MESH)
    for off in (1, -1, 2, -2):
        pl.semaphore_signal(bar, inc=1, device_id={"dp": y_dp(off)}, device_id_type=MESH)
    pl.semaphore_signal(bar, inc=1, device_id={"dp": sibling}, device_id_type=MESH)
    column = y // 2
    at_home = (column == h).astype(jnp.int32)
    for s in range(2):
        for p in range(NX):
            @pl.when((y != 2 * h + s) | (h != p))
            def _():
                pl.semaphore_signal(
                    bar, inc=1, device_id={"dp": (2 * h + s) * 2 + core, "head": p}, device_id_type=MESH
                )

    for copy in loads:
        copy.start()

    tok_rows = tok.shape[0]
    row = lax.broadcasted_iota(jnp.int32, (ROWS, tok_rows), 0)
    block = row >> 4
    slot = row & (CAP - 1)
    size = 8 - ((block + 1) >> 1)
    target = ((e + NZ + jnp.where((block & 1) == 1, size, -size)) & (NZ - 1)) * 8
    loads[0].wait()
    loads[1].wait()
    chosen = jnp.zeros((ROWS, tok_rows), jnp.float32)
    weight = jnp.zeros((ROWS, tok_rows), jnp.float32)
    for i in range(8):
        match = rts[i : i + 1, :] == target
        chosen = jnp.where(match, 1.0, chosen)
        weight = jnp.where(match, rtw[i : i + 1, :], weight)
    upto = (
        lax.broadcasted_iota(jnp.int32, (tok_rows, tok_rows), 0)
        <= lax.broadcasted_iota(jnp.int32, (tok_rows, tok_rows), 1)
    )
    count = jnp.dot(
        chosen.astype(jnp.bfloat16),
        jnp.where(upto, 1.0, 0.0).astype(jnp.bfloat16),
        preferred_element_type=jnp.float32,
    )
    picked = jnp.where(count == (slot + 1).astype(jnp.float32), chosen, 0.0)
    loads[2].wait()
    outbox[...] = jnp.dot(
        picked.astype(jnp.bfloat16), tok[...], preferred_element_type=jnp.float32
    ).astype(jnp.bfloat16)
    loads[3].wait()

    pl.semaphore_wait(bar, (NZ - 1) + 3 + 4 + 1 + NY - at_home)

    def frag_copy(i):
        return pltpu.make_async_remote_copy(
            src_ref=own_down.at[pl.ds(i * FRAG, FRAG)],
            dst_ref=dn.at[core, i, y % 2, h],
            send_sem=fs.at[i],
            recv_sem=fr.at[y % 2, h],
            device_id={"dp": i * 2 + core, "head": column},
            device_id_type=MESH,
        )

    def frag_arrived(s, p):
        pltpu.make_async_remote_copy(
            src_ref=own_down.at[pl.ds(0, FRAG)],
            dst_ref=dn.at[core, y, s, p],
            send_sem=fs.at[0],
            recv_sem=fr.at[s, p],
            device_id={"dp": (2 * h + s) * 2 + core, "head": p},
            device_id_type=MESH,
        ).wait_recv()

    def own_frag():
        return pltpu.make_async_copy(
            own_down.at[pl.ds(pl.multiple_of(y * FRAG, FRAG), FRAG)], dn.at[core, y, y % 2, h], load_sem.at[3]
        )

    def y_copy(block_off, to_off):
        there = y_index(block_off - to_off)
        return pltpu.make_async_remote_copy(
            src_ref=dn.at[core, y_at(block_off)],
            dst_ref=dn.at[core, y_at(block_off)],
            send_sem=ys.at[there],
            recv_sem=yr.at[there],
            device_id={"dp": y_dp(to_off)},
            device_id_type=MESH,
        )

    def y_arrived(off):
        pltpu.make_async_remote_copy(
            src_ref=dn.at[core, y_at(off)],
            dst_ref=dn.at[core, y_at(off)],
            send_sem=ys.at[y_index(off)],
            recv_sem=yr.at[y_index(off)],
            device_id={"dp": y_dp(1)},
            device_id_type=MESH,
        ).wait_recv()

    def core_copy(off):
        i = (off + NY) % NY
        return pltpu.make_async_remote_copy(
            src_ref=dn.at[core, y_at(off)],
            dst_ref=dn.at[core, y_at(off)],
            send_sem=cs.at[i],
            recv_sem=cr.at[i],
            device_id={"dp": sibling},
            device_id_type=MESH,
        )

    def core_arrived(off):
        i = (off + NY) % NY
        pltpu.make_async_remote_copy(
            src_ref=dn.at[1 - core, y_at(off)],
            dst_ref=dn.at[1 - core, y_at(off)],
            send_sem=cs.at[i],
            recv_sem=cr.at[i],
            device_id={"dp": sibling},
            device_id_type=MESH,
        ).wait_recv()

    def z_copy(k):
        return pltpu.make_async_remote_copy(
            src_ref=outbox.at[rows_of(k)],
            dst_ref=arr.at[0, rows_of(k)],
            send_sem=zs.at[k],
            recv_sem=zr.at[k],
            device_id=z_peer(offset_of(k)),
            device_id_type=MESH,
        )

    def x_copy(j, k):
        return pltpu.make_async_remote_copy(
            src_ref=arr.at[0, rows_of(k)],
            dst_ref=arr.at[j + 1, rows_of(k)],
            send_sem=xs.at[j, k],
            recv_sem=xr.at[j, k],
            device_id=x_peer((1, -1, 2)[j]),
            device_id_type=MESH,
        )

    def back_copy(k):
        return pltpu.make_async_remote_copy(
            src_ref=summed.at[rows_of(k)],
            dst_ref=ret.at[rows_of(k)],
            send_sem=bs.at[k],
            recv_sem=br.at[k],
            device_id=z_peer(-offset_of(k)),
            device_id_type=MESH,
        )

    def loop(lo, hi, step):
        def run(k, c):
            step(k)
            return c

        lax.fori_loop(lo, hi, run, 0)

    def spread(k):
        for j in range(3):
            x_copy(j, k).start()

    def pass_on(k):
        z_copy(k).wait_recv()
        spread(k)

    for i in range(NY):
        @pl.when((column != h) | (y != i))
        def _():
            frag_copy(i).start()

    @pl.when(column == h)
    def _():
        own_frag().start()

    loop(EARLY, NZ - 1, lambda k: z_copy(k).start())
    loop(0, EARLY, lambda k: z_copy(k).start())
    arr[0, -CAP:, :] = outbox[-CAP:, :]
    spread(NZ - 1)

    mix = (picked * weight).T
    mix_high = mix.astype(jnp.bfloat16)
    mixing[: tok.shape[0]] = mix_high
    mixing[tok.shape[0] :] = (mix - mix_high.astype(jnp.float32)).astype(jnp.bfloat16)

    def expert_front(g):
        first, last = GROUPS[g]
        n = (last - first) * CAP
        rows = slice(first * CAP, last * CAP)
        gate_act = jnp.zeros((n, wg.shape[2]), jnp.float32)
        up_act = jnp.zeros((n, wg.shape[2]), jnp.float32)
        for r in range(NX):
            if r:
                loop(first, last, lambda k: x_copy(r - 1, k).wait_recv())
            a = arr[r, rows, :]
            gate_act += jnp.dot(a, wg[r], preferred_element_type=jnp.float32)
            up_act += jnp.dot(a, wu[r], preferred_element_type=jnp.float32)
        hidden = gate_act / (1.0 + jnp.exp(-gate_act)) * up_act
        hid[h, rows, :] = hidden.astype(jnp.bfloat16)
        for j in range(3):
            hid_copy(g, j).start()

    def hid_copy(g, j):
        first, last = GROUPS[g]
        rows = pl.ds(first * CAP, (last - first) * CAP)
        return pltpu.make_async_remote_copy(
            src_ref=hid.at[h, rows],
            dst_ref=hid.at[h, rows],
            send_sem=hs.at[g, j],
            recv_sem=hr.at[g, j],
            device_id=x_peer((1, -1, 2)[j]),
            device_id_type=MESH,
        )

    def hid_arrived(g, j):
        first, last = GROUPS[g]
        rows = pl.ds(first * CAP, (last - first) * CAP)
        off = (1, -1, 2)[j]
        source = (h - off + NX) % NX
        pltpu.make_async_remote_copy(
            src_ref=hid.at[source, rows],
            dst_ref=hid.at[source, rows],
            send_sem=hs.at[g, j],
            recv_sem=hr.at[g, j],
            device_id=x_peer(off),
            device_id_type=MESH,
        ).wait_recv()

    def expert_back(groups):
        first, last = GROUPS[groups[0]][0], GROUPS[groups[-1]][1]
        rows = slice(first * CAP, last * CAP)
        for g in groups:
            for j in range(3):
                hid_arrived(g, j)
        for s in range(2):
            for c in range(2):
                value = sum(
                    jnp.dot(
                        hid[p, rows, :],
                        dn[c, :, s, p].reshape(NY * FRAG, dn.shape[-1]),
                        preferred_element_type=jnp.float32,
                    )
                    for p in range(NX)
                )
                b = 2 * s + c
                summed[rows, b * 256 : (b + 1) * 256] = value.astype(jnp.bfloat16)
        loop(first, min(last, NZ - 1), lambda k: back_copy(k).start())

    for s in range(2):
        for p in range(NX):
            @pl.when((y != 2 * h + s) | (h != p))
            def _():
                frag_arrived(s, p)

    @pl.when(column == h)
    def _():
        own_frag().wait()

    y_first = [y_copy(0, off) for off in (2, -2, 1, -1)]
    for copy in y_first:
        copy.start()
    core_copy(0).start()
    loop(EARLY, NZ - 1, pass_on)
    for copy in loads[4:]:
        copy.wait()
    loop(0, 3, pass_on)
    y_arrived(-2)
    y_arrived(2)
    y_second = [y_copy(-2, 2), y_copy(-2, 1), y_copy(2, -1)]
    for copy in y_second:
        copy.start()
    loop(3, 5, pass_on)
    y_arrived(-1)
    y_arrived(1)
    for off in (-1, 1, -2, 2):
        core_copy(off).start()
    loop(5, 7, pass_on)
    expert_front(0)
    for off in (-3, 3, 4):
        y_arrived(off)
        core_copy(off).start()
    loop(7, 11, pass_on)
    for i in range(NY):
        core_arrived(i)
    expert_back((0,))
    expert_front(1)
    loop(11, EARLY, pass_on)
    expert_back((1,))
    expert_front(2)
    expert_back((2,))
    ret[-CAP:, :] = summed[-CAP:, :]

    for i in range(NY):
        @pl.when((column != h) | (y != i))
        def _():
            frag_copy(i).wait_send()
    loop(0, NZ - 1, lambda k: z_copy(k).wait_send())
    for j in range(3):
        loop(0, NZ, lambda k: x_copy(j, k).wait_send())
    for copy in y_first + y_second:
        copy.wait_send()
    for i in range(NY):
        core_copy(i).wait_send()
    for g in range(len(GROUPS)):
        for j in range(3):
            hid_copy(g, j).wait_send()

    def mixed(lo, hi):
        rows = slice(lo * CAP, hi * CAP)
        both = jnp.dot(mixing[:, rows], ret[rows, :], preferred_element_type=jnp.float32)
        return both[: tok.shape[0]] + both[tok.shape[0] :]

    cut = 8
    loop(0, cut, lambda k: back_copy(k).wait_recv())
    total[...] = mixed(0, cut)
    loop(cut, NZ - 1, lambda k: back_copy(k).wait_recv())
    out[...] = (total[...] + mixed(cut, NZ)).astype(jnp.bfloat16)
    loop(0, NZ - 1, lambda k: back_copy(k).wait_send())


def body(tokens, routes, route_weights, gate_weight, up_weight, down_weight):
    tok_rows = tokens.shape[0]
    hidden = gate_weight.shape[2]
    bf16, f32 = jnp.bfloat16, jnp.float32
    dma = pltpu.SemaphoreType.DMA
    groups = len(GROUPS)
    return pl.pallas_call(
        kernel,
        out_shape=jax.ShapeDtypeStruct((tok_rows, QUARTER), bf16),
        in_specs=[pl.BlockSpec(memory_space=pltpu.HBM)] * 6,
        out_specs=pl.BlockSpec(memory_space=pltpu.VMEM),
        scratch_shapes=[
            pltpu.VMEM((tok_rows, QUARTER), bf16),
            pltpu.VMEM((8, tok_rows), jnp.int32),
            pltpu.VMEM((8, tok_rows), f32),
            pltpu.VMEM((NX, QUARTER, hidden), bf16),
            pltpu.VMEM((NX, QUARTER, hidden), bf16),
            pltpu.VMEM((hidden, 256), bf16),
            pltpu.VMEM((2, NY, 2, NX, FRAG, 256), bf16),
            pltpu.VMEM((ROWS, QUARTER), bf16),
            pltpu.VMEM((NX, ROWS, QUARTER), bf16),
            pltpu.VMEM((NX, ROWS, hidden), bf16),
            pltpu.VMEM((ROWS, QUARTER), bf16),
            pltpu.VMEM((ROWS, QUARTER), bf16),
            pltpu.VMEM((2 * tok_rows, ROWS), bf16),
            pltpu.VMEM((tok_rows, QUARTER), f32),
            dma((12,)),
            dma((NZ,)), dma((NZ,)),
            dma((3, NZ)), dma((3, NZ)),
            dma((NY,)), dma((2, NX)),
            dma((7,)), dma((7,)),
            dma((NY,)), dma((NY,)),
            dma((groups, 3)), dma((groups, 3)),
            dma((NZ,)), dma((NZ,)),
        ],
        compiler_params=pltpu.CompilerParams(
            collective_id=0, has_side_effects=True, vmem_limit_bytes=62 * 2**20
        ),
        cost_estimate=pl.CostEstimate(
            flops=2 * ROWS * hidden * 3 * 4096, bytes_accessed=6 * 2**20, transcendentals=ROWS * hidden
        ),
    )(tokens, routes.T, route_weights.T, gate_weight, up_weight, down_weight)


def solution(mesh):
    return jax.shard_map(
        body,
        mesh=mesh,
        in_specs=(
            P(("dp", "expert"), None),
            P(("dp", "expert"), None),
            P(("dp", "expert"), None),
            P("expert", None, "head"),
            P("expert", None, "head"),
            P("expert", "head", "dp"),
        ),
        out_specs=P(("dp", "expert"), "head"),
        check_vma=False,
    )
```
